32 devices in a mesh: blk: 8 (over y, x, core), grp: 4 (over z).
Axes of the slice: x: 2, y: 2, z: 4, core: 2. Of those that a mesh axis runs over, the one named last changes fastest.
Arguments:
- source_emb: float32 [8, 512, 400], P('blk', 'grp'), may hold values from -1.2 to 1.2
- source_state: float32 [8, 512], P('blk', 'grp'), may hold values from 0.01 to 0.1
- target_emb: float32 [8, 512, 400], P('blk', 'grp'), may hold values from -1.2 to 1.2
- target_state: float32 [8, 512], P('blk', 'grp'), may hold values from 0.01 to 0.1
- relation_emb: float32 [512, 400], replicated, may hold values from 0.1 to 1.9
- relation_state: float32 [512], replicated, may hold values from 0.01 to 0.1
- source_ids: int32 [2, 8, 4, 512], P(None, 'blk', 'grp'), may hold values from 0 to 127
- target_ids: int32 [2, 8, 4, 512], P(None, 'blk', 'grp'), may hold values from 0 to 127
- relation_ids: int32 [2, 8, 4, 512], P(None, 'blk', 'grp'), may hold values from 0 to 511
- edge_counts: int32 [2, 8, 4], P(None, 'blk', 'grp'), may hold values from 128 to 512, as said below
- sample_ids: int32 [2, 8, 4, 1, 256], P(None, 'blk', 'grp'), may hold values from 0 to 127
Outputs:
- source_out: float32 [8, 512, 400], P('blk', 'grp')
- source_state_out: float32 [8, 512], P('blk', 'grp')
- target_out: float32 [8, 512, 400], P('blk', 'grp')
- target_state_out: float32 [8, 512], P('blk', 'grp')
- relation_out: float32 [512, 400], replicated
- relation_state_out: float32 [512], replicated
The draws below stay inside these ranges and needn't reach their ends.
Inputs may be any that keep to these rules, and one draw needn't show every extreme that they name: `edge_counts`: in every round some bucket is full.
All inputs are finite; a program needn't handle non-finite values.
Results may differ from the reference program's by a relative error of at most 0.0003.
Values sent between devices are 32-bit elements; how exact they have to be, the bound alone decides.
A program may use at most 64 MiB of HBM per device.

```python
import math
import jax
import jax.numpy as jnp
import numpy as np
from jax import lax

D = 400
RELATIONS = 512
ROWS_DEV = 128
NEGATIVES = 256
BLOCKS = 1
ROUNDS = 2
EDGE_SLOTS = 512
PARTS_SIZE = 8
GROUPS = 4
ROWS = 512


def draw_edge_counts(key, part):
    key = jax.random.fold_in(key, 11)
    first_key, second_key = jax.random.split(key)
    dims_shape = (ROUNDS, PARTS_SIZE, GROUPS)
    counted = jax.random.randint(first_key, dims_shape, EDGE_SLOTS // 4, EDGE_SLOTS + 1)
    chosen = jax.random.randint(second_key, (ROUNDS, 1, 1), 0, PARTS_SIZE * GROUPS)
    position = lax.broadcasted_iota(jnp.int32, dims_shape, 1) * GROUPS + lax.broadcasted_iota(jnp.int32, dims_shape, 2)
    return jnp.where(position == chosen, EDGE_SLOTS, counted).astype(jnp.int32)


def place_ends(values, key, least, top_value):
    longest = values.shape.index(max(values.shape))
    spots = []
    for shift in (0, 1):
        where = [jax.random.randint(jax.random.fold_in(key, axis), (), 0, length) for axis, length in enumerate(values.shape)]
        where[longest] = (where[longest] + shift) % values.shape[longest]
        spots.append(tuple(where))
    return values.at[spots[0]].set(least).at[spots[1]].set(top_value)


def block_scale(own_key, extent, cuts, least, high):
    level, own = 1.0, jax.random.fold_in(own_key, 6)
    for dim, shards_of in cuts:
        draws = jnp.exp(jax.random.uniform(jax.random.fold_in(own, dim), (shards_of,), jnp.float32, least / len(cuts), high / len(cuts)))
        level = level * jnp.repeat(draws, extent[dim] // shards_of).reshape([-1 if axis == dim else 1 for axis in range(len(extent))])
    return level


def rank_table(count, lean):
    portions = [(1 << 20) // math.isqrt(grade ** lean) + 1 for grade in range(1, count + 1)]
    deviation = 1 + sum(portions) // (1 << 30)
    return np.cumsum(np.array([max(1, weight // deviation) for weight in portions]))


def skewed_ids(rng, shape, amount, slope):
    table = rank_table(amount, slope)
    pick = jax.random.randint(jax.random.fold_in(rng, 1), shape, 0, int(table[amount - 1]))
    rank = jnp.searchsorted(jnp.asarray(table, jnp.int32), pick, side="right")
    return jax.random.permutation(jax.random.fold_in(rng, 2), amount)[rank].astype(jnp.int32)


def bell_draw(key, dims, deviation, limit, shards=(), kind=jnp.bfloat16):
    entries = deviation * jax.random.normal(key, dims, jnp.float32)
    if shards:
        entries = entries * block_scale(key, dims, shards, -0.22, 0.18)
    return jnp.clip(entries, -limit, limit).astype(kind)


def setup_inputs(seed: int = 0) -> dict:
    streams_of = jax.random.split(jax.random.key(seed), 12)
    return {
        "source_emb": bell_draw(streams_of[0], (PARTS_SIZE, ROWS, D), 0.2, 1.2, ((0, 8), (1, 4)), jnp.float32),
        "source_state": jnp.clip(jnp.exp(math.log(0.1) - 2.3025851 * jax.random.uniform(streams_of[1], (PARTS_SIZE, ROWS), jnp.float32) ** block_scale(streams_of[1], (PARTS_SIZE, ROWS), ((0, 8), (1, 4)), -0.2, 0.2)), 0.01, 0.1),
        "target_emb": bell_draw(streams_of[2], (PARTS_SIZE, ROWS, D), 0.2, 1.2, ((0, 8), (1, 4)), jnp.float32),
        "target_state": jnp.clip(jnp.exp(math.log(0.1) - 2.3025851 * jax.random.uniform(streams_of[3], (PARTS_SIZE, ROWS), jnp.float32) ** block_scale(streams_of[3], (PARTS_SIZE, ROWS), ((0, 8), (1, 4)), -0.2, 0.2)), 0.01, 0.1),
        "relation_emb": jnp.clip(1.0 + 0.18 * jax.random.normal(streams_of[4], (RELATIONS, D), jnp.float32), 0.1, 1.9),
        "relation_state": jnp.clip(jnp.exp(jax.random.uniform(streams_of[5], (RELATIONS,), jnp.float32, math.log(0.01), math.log(0.1))), 0.01, 0.1),
        "source_ids": place_ends(jax.random.randint(streams_of[6], (ROUNDS, PARTS_SIZE, GROUPS, EDGE_SLOTS), 0, ROWS_DEV), jax.random.fold_in(streams_of[6], 1), 0, ROWS_DEV - 1).astype(jnp.int32),
        "target_ids": place_ends(jax.random.randint(streams_of[7], (ROUNDS, PARTS_SIZE, GROUPS, EDGE_SLOTS), 0, ROWS_DEV), jax.random.fold_in(streams_of[7], 1), 0, ROWS_DEV - 1).astype(jnp.int32),
        "relation_ids": place_ends(skewed_ids(streams_of[8], (ROUNDS, PARTS_SIZE, GROUPS, EDGE_SLOTS), RELATIONS, 2), jax.random.fold_in(streams_of[8], 3), 0, RELATIONS - 1).astype(jnp.int32),
        "edge_counts": draw_edge_counts(jax.random.fold_in(streams_of[11], 71), 0),
        "sample_ids": place_ends(jax.random.randint(streams_of[10], (ROUNDS, PARTS_SIZE, GROUPS, BLOCKS, NEGATIVES), 0, ROWS_DEV), jax.random.fold_in(streams_of[10], 1), 0, ROWS_DEV - 1).astype(jnp.int32),
    }


learning_rate = 0.1
relation_rate = 0.1

def adagrad(weights, accum, grads, rate):
    fresh = accum + lax.optimization_barrier(jnp.mean(grads * grads, axis=-1))
    return (weights - rate * grads * lax.rsqrt(fresh)[..., None], fresh)

def bucket(source_rows, target_rows, relation, source_idx, target_idx, kind_idx, live_count, sample_idx):
    slots = source_idx.shape[0]
    blocks, samples = sample_idx.shape
    per_block = slots // blocks
    width = source_rows.shape[1]
    nrows = source_rows.shape[0]
    alive = (jnp.arange(slots, dtype=jnp.int32) < live_count).astype(jnp.float32)
    left = source_rows[source_idx]
    right = target_rows[target_idx]
    scale = relation[kind_idx]
    query = left * scale
    positive = lax.optimization_barrier(jnp.sum(query * right, axis=-1))
    sampled = target_rows[sample_idx]
    blocked = query.reshape(blocks, per_block, width)
    negative = jnp.einsum('bid,bjd->bij', blocked, sampled, precision=lax.Precision.HIGHEST)
    pull = -alive * jax.nn.sigmoid(-positive)
    push = alive.reshape(blocks, per_block, 1) * jax.nn.sigmoid(negative) / samples
    grad_query = pull[:, None] * right + jnp.einsum('bij,bjd->bid', push, sampled, precision=lax.Precision.HIGHEST).reshape(slots, width)
    grad_source = jax.ops.segment_sum(grad_query * scale, source_idx, num_segments=nrows)
    to_samples = jnp.einsum('bij,bid->bjd', push, blocked, precision=lax.Precision.HIGHEST).reshape(-1, width)
    grad_target = jax.ops.segment_sum(pull[:, None] * query, target_idx, num_segments=nrows)
    grad_target = grad_target + jax.ops.segment_sum(to_samples, sample_idx.reshape(-1), num_segments=nrows)
    grad_relation = jax.ops.segment_sum(grad_query * left, kind_idx, num_segments=relation.shape[0])
    return (grad_source, grad_target, grad_relation)

def reference(source_emb, source_state, target_emb, target_state, relation_emb, relation_state, source_ids, target_ids, relation_ids, edge_counts, sample_ids):
    parts = source_emb.shape[0]
    slabs = parts * GROUPS
    width = source_emb.shape[2]
    source_rows = source_emb.reshape(slabs, ROWS_DEV, width)
    source_acc = source_state.reshape(slabs, ROWS_DEV)
    target_rows = target_emb.reshape(slabs, ROWS_DEV, width)
    target_acc = target_state.reshape(slabs, ROWS_DEV)
    flat_source = source_ids.reshape(ROUNDS, slabs, -1)
    flat_target = target_ids.reshape(ROUNDS, slabs, -1)
    flat_kind = relation_ids.reshape(ROUNDS, slabs, -1)
    flat_count = edge_counts.reshape(ROUNDS, slabs)
    flat_sample = sample_ids.reshape(ROUNDS, slabs, BLOCKS, NEGATIVES)
    total = jnp.zeros(relation_emb.shape, jnp.float32)
    for round_index in range(ROUNDS):

        def visit(running, inputs):
            grad_source, grad_target, grad_relation = bucket(inputs[0], inputs[1], relation_emb, inputs[2], inputs[3], inputs[4], inputs[5], inputs[6])
            return (running + grad_relation, (grad_source, grad_target))
        total, grads = lax.scan(visit, total, (source_rows, target_rows, flat_source[round_index], flat_target[round_index], flat_kind[round_index], flat_count[round_index], flat_sample[round_index]))
        target_rows, target_acc = adagrad(target_rows, target_acc, grads[1], learning_rate)
        source_rows, source_acc = adagrad(source_rows, source_acc, grads[0], learning_rate)
        if round_index + 1 < ROUNDS:
            source_rows = jnp.roll(source_rows.reshape(parts, GROUPS, ROWS_DEV, width), 1, axis=0).reshape(slabs, ROWS_DEV, width)
            source_acc = jnp.roll(source_acc.reshape(parts, GROUPS, ROWS_DEV), 1, axis=0).reshape(slabs, ROWS_DEV)
    relation_out, relation_state_out = adagrad(relation_emb, relation_state, total, relation_rate)
    return (source_rows.reshape(source_emb.shape), source_acc.reshape(source_state.shape), target_rows.reshape(target_emb.shape), target_acc.reshape(target_state.shape), relation_out, relation_state_out)
```

```python
import functools

import jax
import jax.numpy as jnp
from jax import lax
from jax.experimental import pallas as pl
from jax.experimental.pallas import tpu as pltpu
from jax.sharding import PartitionSpec as P

RATE = 0.1
SUBLANES = 8
MESH = pl.DeviceIdType.MESH
BF16 = jnp.bfloat16
F32 = jnp.float32


def halves_of(x):
    high = x.astype(BF16)
    return high, (x - high.astype(F32)).astype(BF16)


def mm(a, b):
    return jnp.dot(a, b, preferred_element_type=F32)


def mm_nt(a, b):
    return lax.dot_general(a, b, (((1,), (1,)), ((), ())), preferred_element_type=F32)


def adagrad(weights, sums, grads):
    fresh = sums + jnp.sum(grads * grads, axis=0, keepdims=True) * (1.0 / grads.shape[0])
    return weights - RATE * grads * lax.rsqrt(fresh), fresh


def plan(n, m, width):
    steps = []
    tiles = width // SUBLANES
    for _ in range(1, n.bit_length() - 1):
        each, both = tiles // 2, tiles % 2
        steps.append((each, both))
        tiles = each + both
    return steps, (tiles // m, tiles % m)


def copy_count(n, m, width, rounds):
    steps, (each, both) = plan(n, m, width)
    out = 2 * sum(1 for step in steps if step[0]) + 2 * (m - 1) * (each > 0)
    back = 2 * (m - 1) * ((each > 0) + (both > 0))
    return (rounds - 1) + 2 + 2 * len(steps) + back + out + 2


def kernel(
    n,
    m,
    source_ref,
    source_state_ref,
    target_ref,
    target_state_ref,
    relation_ref,
    relation_state_ref,
    source_ids_ref,
    target_ids_ref,
    relation_ids_ref,
    counts_ref,
    samples_ref,
    source_out,
    source_state_out,
    target_out,
    target_state_out,
    relation_out,
    relation_state_out,
    hot_ref,
    grads,
    result,
    slab_send,
    slab_recv,
    first_recv,
    step_recv,
    grp_recv,
    send_sem,
    recv_sem,
):
    blk, grp = lax.axis_index("blk"), lax.axis_index("grp")
    bits = n.bit_length() - 1
    rounds = source_ids_ref.shape[0]
    slots = source_ids_ref.shape[3]
    samples = samples_ref.shape[4]
    width, rows = source_ref.shape[1:]
    kinds = relation_ref.shape[1]
    quarter = kinds // 4
    steps, (grp_each, grp_both) = plan(n, m, width)
    after, before = lax.rem(blk + 1, n), lax.rem(blk + n - 1, n)

    def bit_of(bit):
        return lax.rem(blk // (1 << bit), 2)

    def flipped(bit):
        return blk + (1 << bit) - 2 * (1 << bit) * bit_of(bit)

    barrier = pltpu.get_barrier_semaphore()
    greeted = [(after, grp), (before, grp)]
    greeted += [(flipped(bit), grp) for bit in range(bits)]
    greeted += [(blk, lax.rem(grp + step, m)) for step in range(1, m)]
    for where in greeted:
        pl.semaphore_signal(barrier, inc=1, device_id=where, device_id_type=MESH)

    started, sent = [], []

    def send(src, dst, where):
        copy = pltpu.make_async_remote_copy(
            src_ref=src,
            dst_ref=dst,
            send_sem=send_sem.at[len(started)],
            recv_sem=recv_sem.at[len(started)],
            device_id=where,
            device_id_type=MESH,
        )
        copy.start()
        started.append(copy)
        return copy

    table_high, table_low = halves_of(relation_ref[...])

    def relation_side(index):
        picked = relation_ids_ref[index, 0]
        hot = (lax.broadcasted_iota(jnp.int32, (kinds, slots), 0) == picked).astype(BF16)
        hot_ref[index] = hot
        return mm(table_high, hot) + mm(table_low, hot)

    def edge_side(index):
        row_iota = lax.broadcasted_iota(jnp.int32, (rows, slots), 0)
        source_hot = (row_iota == source_ids_ref[index, 0]).astype(BF16)
        target_hot = row_iota == target_ids_ref[index, 0]
        sample_iota = lax.broadcasted_iota(jnp.int32, (rows, samples), 0)
        named = (sample_iota == samples_ref[index, 0, 0]).astype(F32)
        share = jnp.sum(named, axis=1, keepdims=True) * (1.0 / samples)
        alive = (
            lax.broadcasted_iota(jnp.int32, (1, slots), 1) < counts_ref[0, 0, index]
        ).astype(F32)
        return source_hot, target_hot, share, alive

    source, source_sums = source_ref[0], source_state_ref[...]
    target, target_sums = target_ref[0], target_state_ref[...]
    scale = relation_side(0)
    edges = edge_side(0)
    pl.semaphore_wait(barrier, len(greeted))

    for index in range(rounds):
        source_hot, target_hot, share, alive = edges
        source_high, source_low = halves_of(source)
        left = mm(source_high, source_hot) + mm(source_low, source_hot)
        query = left * scale
        query_high, query_low = halves_of(query)
        flat_high, flat_low = halves_of(target.T)
        logits = mm(flat_high, query_high) + (
            mm(flat_low, query_high) + mm(flat_high, query_low)
        )
        positive = jnp.sum(jnp.where(target_hot, logits, 0.0), axis=0, keepdims=True)
        pull = -alive * jax.nn.sigmoid(-positive)
        push = share * alive * jax.nn.sigmoid(logits)
        weight = jnp.where(target_hot, pull, 0.0) + push
        weight_high, weight_low = halves_of(weight)
        target_high, target_low = halves_of(target)
        grad_query = mm(target_high, weight_high) + (
            mm(target_low, weight_high) + mm(target_high, weight_low)
        )

        def source_step():
            high, low = halves_of(grad_query * scale)
            fresh = mm_nt(high, source_hot) + mm_nt(low, source_hot)
            return adagrad(source, source_sums, fresh)

        def target_step():
            fresh = mm_nt(query_high, weight_high) + (
                mm_nt(query_high, weight_low) + mm_nt(query_low, weight_high)
            )
            return adagrad(target, target_sums, fresh)

        def relation_part(core):
            high, low = halves_of(grad_query * left)
            hot = hot_ref[index, pl.ds(pl.multiple_of(core * 2 * quarter, quarter), 2 * quarter)]
            fresh = mm_nt(high, hot) + mm_nt(low, hot)
            for part in range(2):
                piece = fresh[:, part * quarter : (part + 1) * quarter]
                if index == 0:
                    grads[core, part] = piece
                else:
                    grads[core, part] += piece

        if index + 1 < rounds:
            new_source, new_sums = source_step()
            slab_send[index, :width] = new_source
            slab_send[index, width:] = jnp.broadcast_to(new_sums, (SUBLANES, rows))
            copy = send(slab_send.at[index], slab_recv.at[index], (after, grp))
            new_target, new_target_sums = target_step()
            relation_part(0)
            relation_part(1)
            scale = relation_side(index + 1)
            edges = edge_side(index + 1)
            target, target_sums = new_target, new_target_sums
            copy.wait_recv()
            source = slab_recv[index, :width]
            source_sums = slab_recv[index, width : width + 1]

    mine = bit_of(0)
    core = (flipped(0), grp)
    relation_part(1 - mine)
    first_copies = [
        send(grads.at[1 - mine, part], first_recv.at[part], core) for part in range(2)
    ]
    relation_part(mine)
    new_source, new_sums = source_step()
    source_out[0] = new_source
    source_state_out[...] = new_sums

    orders = [list(range(1, bits)), list(range(bits - 1, 0, -1))]
    bases = [0, 0]
    history = [[], []]
    pending = [None, None]
    grp_copies = [[], []]

    def span(base, tiles):
        return pl.ds(pl.multiple_of(base * SUBLANES, SUBLANES), tiles * SUBLANES)

    def piece(part, base, tiles):
        return grads.at[mine, part, span(base, tiles)]

    def launch(part, step):
        each, both = steps[step]
        bit = orders[part][step]
        high = bit_of(bit)
        base = bases[part]
        where = (flipped(bit), grp)
        pending[part] = send(
            piece(part, base + (1 - high) * each, each + both),
            step_recv.at[part, step, pl.ds(0, (each + both) * SUBLANES)],
            where,
        )
        history[part].append((where, base, base + high * (each + both), each))
        bases[part] = base + high * each

    def launch_grp(part):
        base = bases[part]
        for step in range(1, m):
            peer = lax.rem(grp + step, m)
            if grp_each:
                copy = send(
                    piece(part, base + peer * grp_each, grp_each),
                    grp_recv.at[part, step - 1, pl.ds(0, grp_each * SUBLANES)],
                    (blk, peer),
                )
                grp_copies[part].append(copy)
            if grp_both:
                copy = send(
                    piece(part, base + m * grp_each, grp_both),
                    grp_recv.at[
                        part, step - 1, pl.ds(grp_each * SUBLANES, grp_both * SUBLANES)
                    ],
                    (blk, peer),
                )
                grp_copies[part].append(copy)

    def advance(part, step):
        if step < len(steps):
            launch(part, step)
        else:
            launch_grp(part)

    for part in range(2):
        first_copies[part].wait_recv()
        grads[mine, part] += first_recv[part]
        advance(part, 0)
    new_target, new_target_sums = target_step()
    target_out[0] = new_target
    target_state_out[...] = new_target_sums
    for step in range(len(steps)):
        each, both = steps[step]
        for part in range(2):
            pending[part].wait_recv()
            if both:
                pending[part].wait_send()
                sent.append(id(pending[part]))
            where = span(bases[part], each + both)
            grads[mine, part, where] += step_recv[part, step, : (each + both) * SUBLANES]
            advance(part, step + 1)

    def summed(part, base, first, tiles):
        own = grads[mine, part, span(base, tiles)]
        total = None
        for member in range(m):
            slot = lax.max(lax.rem(grp - member + m, m) - 1, 0)
            came = grp_recv[part, slot, first * SUBLANES : (first + tiles) * SUBLANES]
            term = jnp.where(grp == member, own, came)
            total = term if total is None else total + term
        result[mine, part, span(base, tiles)] = total

    out_pending = [[], []]
    for part in range(2):
        for copy in grp_copies[part]:
            copy.wait_recv()
        base = bases[part]
        if grp_both:
            summed(part, base + m * grp_each, grp_each, grp_both)
        if grp_each:
            summed(part, base + grp * grp_each, 0, grp_each)
            for step in range(1, m):
                ref = result.at[mine, part, span(base + grp * grp_each, grp_each)]
                out_pending[part].append(send(ref, ref, (blk, lax.rem(grp + step, m))))
    for back in range(len(steps) - 1, -1, -1):
        for part in range(2):
            where, base, first, each = history[part][back]
            for copy in out_pending[part]:
                copy.wait_recv()
            out_pending[part] = []
            if each:
                ref = result.at[mine, part, span(first, each)]
                out_pending[part] = [send(ref, ref, where)]
    for part in range(2):
        for copy in out_pending[part]:
            copy.wait_recv()
        ref = result.at[mine, part]
        out_pending[part] = [send(ref, ref, core)]
    for part in range(2):
        out_pending[part][0].wait_recv()
    for side in range(2):
        for part in range(2):
            lanes = slice((2 * side + part) * quarter, (2 * side + part + 1) * quarter)
            fresh, sums = adagrad(
                relation_ref[:, lanes], relation_state_ref[:, lanes], result[side, part]
            )
            relation_out[:, lanes] = fresh
            relation_state_out[:, lanes] = sums
    for copy in started:
        if id(copy) not in sent:
            copy.wait_send()


def on_device(n, m, *arrays):
    arrays = list(arrays)
    rounds, slots = arrays[6].shape[0], arrays[6].shape[3]
    kinds, width = arrays[4].shape
    rows = arrays[0].shape[1]
    arrays[0] = jnp.swapaxes(arrays[0], 1, 2)
    arrays[2] = jnp.swapaxes(arrays[2], 1, 2)
    arrays[4] = arrays[4].T
    arrays[5] = arrays[5].reshape(1, kinds)
    arrays[9] = jnp.transpose(arrays[9], (1, 2, 0))
    quarter = kinds // 4
    steps, (grp_each, grp_both) = plan(n, m, width)
    copies = copy_count(n, m, width, rounds)
    largest = SUBLANES * sum(steps[0])
    slab = (max(rounds - 1, 1), width + SUBLANES, rows)
    vmem = pl.BlockSpec(memory_space=pltpu.VMEM)
    smem = pl.BlockSpec(memory_space=pltpu.SMEM)
    outs = pl.pallas_call(
        functools.partial(kernel, n, m),
        out_shape=[jax.ShapeDtypeStruct(a.shape, F32) for a in arrays[:6]],
        in_specs=[vmem] * 9 + [smem, vmem],
        out_specs=[vmem] * 6,
        scratch_shapes=[
            pltpu.VMEM((rounds, kinds, slots), BF16),
            pltpu.VMEM((2, 2, width, quarter), F32),
            pltpu.VMEM((2, 2, width, quarter), F32),
            pltpu.VMEM(slab, F32),
            pltpu.VMEM(slab, F32),
            pltpu.VMEM((2, width, quarter), F32),
            pltpu.VMEM((2, len(steps), largest, quarter), F32),
            pltpu.VMEM((2, m - 1, (grp_each + grp_both) * SUBLANES, quarter), F32),
            pltpu.SemaphoreType.DMA((copies,)),
            pltpu.SemaphoreType.DMA((copies,)),
        ],
        compiler_params=pltpu.CompilerParams(
            collective_id=0, has_side_effects=True, vmem_limit_bytes=40 * 2**20
        ),
        name="train",
    )(*arrays)
    return (
        jnp.swapaxes(outs[0], 1, 2),
        outs[1],
        jnp.swapaxes(outs[2], 1, 2),
        outs[3],
        outs[4].T,
        outs[5].reshape(kinds),
    )


def solution(mesh):
    n, m = mesh.shape["blk"], mesh.shape["grp"]
    in_specs = (
        P("blk", "grp", None),
        P("blk", "grp"),
        P("blk", "grp", None),
        P("blk", "grp"),
        P(),
        P(),
        P(None, "blk", "grp", None),
        P(None, "blk", "grp", None),
        P(None, "blk", "grp", None),
        P(None, "blk", "grp"),
        P(None, "blk", "grp", None, None),
    )
    out_specs = (
        P("blk", "grp", None),
        P("blk", "grp"),
        P("blk", "grp", None),
        P("blk", "grp"),
        P(),
        P(),
    )
    return jax.shard_map(
        functools.partial(on_device, n, m),
        mesh=mesh,
        in_specs=in_specs,
        out_specs=out_specs,
        check_vma=False,
    )
```

```python
import functools

import jax
import jax.numpy as jnp
from jax import lax
from jax.experimental import pallas as pl
from jax.experimental.pallas import tpu as pltpu
from jax.sharding import PartitionSpec as P

RATE = 0.1
SUBLANES = 8
MESH = pl.DeviceIdType.MESH
BF16 = jnp.bfloat16
F32 = jnp.float32
done = object()


def halves_of(x):
    high = x.astype(BF16)
    return high, (x - high.astype(F32)).astype(BF16)


def mm(a, b):
    return jnp.dot(a, b, preferred_element_type=F32)


def mm_nt(a, b):
    return lax.dot_general(a, b, (((1,), (1,)), ((), ())), preferred_element_type=F32)


def adagrad(weights, sums, grads):
    fresh = sums + jnp.sum(grads * grads, axis=0, keepdims=True) * (1.0 / grads.shape[0])
    return weights - RATE * grads * lax.rsqrt(fresh), fresh


def chunks_of(width):
    tiles = width // SUBLANES
    large = 1 << (tiles.bit_length() - 1)
    return [(0, large), (large, tiles - large)] if large < tiles else [(0, tiles)]


def plan(n, m, tiles):
    steps = []
    for _ in range(1, n.bit_length() - 1):
        each, both = tiles // 2, tiles % 2
        steps.append((each, both))
        tiles = each + both
    return steps, (tiles // m, tiles % m)


def copy_count(n, m, width, rounds):
    count = rounds - 1
    for _, tiles in chunks_of(width):
        steps, (each, both) = plan(n, m, tiles)
        unit = 2 + len(steps) + sum(1 for step in steps if step[0])
        unit += (m - 1) * (2 * (each > 0) + (both > 0))
        count += 2 * unit
    return count


def kernel(n, m, *refs):
    hbm, refs = refs[:11], refs[11:]
    outs, refs = refs[:6], refs[6:]
    staged, refs = refs[:11], refs[11:]
    inner(n, m, hbm, *staged, *outs, *refs)


def inner(
    n,
    m,
    hbm,
    source_ref,
    source_state_ref,
    target_ref,
    target_state_ref,
    relation_ref,
    relation_state_ref,
    source_ids_ref,
    target_ids_ref,
    relation_ids_ref,
    counts_ref,
    samples_ref,
    source_out,
    source_state_out,
    target_out,
    target_state_out,
    relation_out,
    relation_state_out,
    hot_ref,
    grads,
    result,
    slab_send,
    slab_recv,
    first_recv,
    step_recv,
    grp_recv,
    send_sem,
    recv_sem,
    load_sem,
):
    staged = (
        source_ref,
        source_state_ref,
        target_ref,
        target_state_ref,
        relation_ref,
        relation_state_ref,
        source_ids_ref,
        target_ids_ref,
        relation_ids_ref,
        counts_ref,
        samples_ref,
    )
    loads = [
        pltpu.make_async_copy(src, dst, load_sem.at[number])
        for number, (src, dst) in enumerate(zip(hbm, staged))
    ]
    for number in (4, 8, 0, 6, 2, 7, 10, 9, 1, 3, 5):
        loads[number].start()
    blk, grp = lax.axis_index("blk"), lax.axis_index("grp")
    bits = n.bit_length() - 1
    rounds = source_ids_ref.shape[0]
    slots = source_ids_ref.shape[3]
    samples = samples_ref.shape[4]
    width, rows = source_ref.shape[1:]
    kinds = relation_ref.shape[1]
    quarter = kinds // 4
    after, before = lax.rem(blk + 1, n), lax.rem(blk + n - 1, n)

    def bit_of(bit):
        return lax.rem(blk // (1 << bit), 2)

    def flipped(bit):
        return blk + (1 << bit) - 2 * (1 << bit) * bit_of(bit)

    barrier = pltpu.get_barrier_semaphore()
    greeted = [(after, grp), (before, grp)]
    greeted += [(flipped(bit), grp) for bit in range(bits)]
    greeted += [(blk, lax.rem(grp + step, m)) for step in range(1, m)]
    for where in greeted:
        pl.semaphore_signal(barrier, inc=1, device_id=where, device_id_type=MESH)

    started, sent = [], []

    def send(src, dst, where):
        copy = pltpu.make_async_remote_copy(
            src_ref=src,
            dst_ref=dst,
            send_sem=send_sem.at[len(started)],
            recv_sem=recv_sem.at[len(started)],
            device_id=where,
            device_id_type=MESH,
        )
        copy.start()
        started.append(copy)
        return copy

    loads[4].wait()
    table_high, table_low = halves_of(relation_ref[...])

    def relation_side(index):
        picked = relation_ids_ref[index, 0]
        hot = (lax.broadcasted_iota(jnp.int32, (kinds, slots), 0) == picked).astype(BF16)
        hot_ref[index] = hot
        return mm(table_high, hot) + mm(table_low, hot)

    def edge_side(index):
        row_iota = lax.broadcasted_iota(jnp.int32, (rows, slots), 0)
        source_hot = (row_iota == source_ids_ref[index, 0]).astype(BF16)
        target_hot = row_iota == target_ids_ref[index, 0]
        sample_iota = lax.broadcasted_iota(jnp.int32, (rows, samples), 0)
        named = (sample_iota == samples_ref[index, 0, 0]).astype(F32)
        share = jnp.sum(named, axis=1, keepdims=True) * (1.0 / samples)
        alive = (
            lax.broadcasted_iota(jnp.int32, (1, slots), 1) < counts_ref[0, 0, index]
        ).astype(F32)
        return source_hot, target_hot, share, alive

    loads[8].wait()
    scale = relation_side(0)
    for number in (0, 6, 2, 7, 10, 9, 1, 3, 5):
        loads[number].wait()
    source, source_sums = source_ref[0], source_state_ref[...]
    target, target_sums = target_ref[0], target_state_ref[...]
    edges = edge_side(0)
    pl.semaphore_wait(barrier, len(greeted))

    for index in range(rounds):
        source_hot, target_hot, share, alive = edges
        source_high, source_low = halves_of(source)
        left = mm(source_high, source_hot) + mm(source_low, source_hot)
        query = left * scale
        query_high, query_low = halves_of(query)
        flat_high, flat_low = halves_of(target.T)
        logits = mm(flat_high, query_high) + (
            mm(flat_low, query_high) + mm(flat_high, query_low)
        )
        positive = jnp.sum(jnp.where(target_hot, logits, 0.0), axis=0, keepdims=True)
        pull = -alive * jax.nn.sigmoid(-positive)
        push = share * alive * jax.nn.sigmoid(logits)
        weight = jnp.where(target_hot, pull, 0.0) + push
        weight_high, weight_low = halves_of(weight)
        target_high, target_low = halves_of(target)
        grad_query = mm(target_high, weight_high) + (
            mm(target_low, weight_high) + mm(target_high, weight_low)
        )

        def source_step():
            high, low = halves_of(grad_query * scale)
            fresh = mm_nt(high, source_hot) + mm_nt(low, source_hot)
            return adagrad(source, source_sums, fresh)

        def target_step():
            fresh = mm_nt(query_high, weight_high) + (
                mm_nt(query_high, weight_low) + mm_nt(query_low, weight_high)
            )
            return adagrad(target, target_sums, fresh)

        relation_high, relation_low = halves_of(grad_query * left)

        def relation_part(core):
            hot = hot_ref[index, pl.ds(pl.multiple_of(core * 2 * quarter, quarter), 2 * quarter)]
            fresh = mm_nt(relation_high, hot) + mm_nt(relation_low, hot)
            for part in range(2):
                piece = fresh[:, part * quarter : (part + 1) * quarter]
                if index == 0:
                    grads[core, part] = piece
                else:
                    grads[core, part] += piece

        if index + 1 < rounds:
            new_source, new_sums = source_step()
            slab_send[index, :width] = new_source
            slab_send[index, width:] = jnp.broadcast_to(new_sums, (SUBLANES, rows))
            copy = send(slab_send.at[index], slab_recv.at[index], (after, grp))
            new_target, new_target_sums = target_step()
            relation_part(0)
            relation_part(1)
            scale = relation_side(index + 1)
            edges = edge_side(index + 1)
            target, target_sums = new_target, new_target_sums
            copy.wait_recv()
            source = slab_recv[index, :width]
            source_sums = slab_recv[index, width : width + 1]

    mine = bit_of(0)
    core = (flipped(0), grp)
    orders = [list(range(1, bits)), list(range(bits - 1, 0, -1))]

    def span(base, tiles):
        return pl.ds(pl.multiple_of(base * SUBLANES, SUBLANES), tiles * SUBLANES)

    def summed(part, chunk, base, first, tiles):
        own = grads[mine, part, span(base, tiles)]
        total = None
        for member in range(m):
            slot = lax.max(lax.rem(grp - member + m, m) - 1, 0)
            came = grp_recv[
                chunk, part, slot, first * SUBLANES : (first + tiles) * SUBLANES
            ]
            term = jnp.where(grp == member, own, came)
            total = term if total is None else total + term
        result[mine, part, span(base, tiles)] = total

    def reduce_unit(part, chunk, start, tiles):
        steps, (grp_each, grp_both) = plan(n, m, tiles)
        where = span(start, tiles)
        copy = send(
            grads.at[1 - mine, part, where], first_recv.at[part, where], core
        )
        yield
        copy.wait_recv()
        grads[mine, part, where] += first_recv[part, where]
        base, history = start, []
        for number, (each, both) in enumerate(steps):
            bit = orders[part][number]
            high = bit_of(bit)
            partner = (flipped(bit), grp)
            size = each + both
            copy = send(
                grads.at[mine, part, span(base + (1 - high) * each, size)],
                step_recv.at[chunk, part, number, pl.ds(0, size * SUBLANES)],
                partner,
            )
            history.append((partner, base + high * size, each))
            base = base + high * each
            yield
            copy.wait_recv()
            if both:
                copy.wait_send()
                sent.append(id(copy))
            came = step_recv[chunk, part, number, : size * SUBLANES]
            grads[mine, part, span(base, size)] += came
        copies = []
        for step in range(1, m):
            peer = lax.rem(grp + step, m)
            pieces = [(base + peer * grp_each, 0, grp_each)]
            pieces += [(base + m * grp_each, grp_each, grp_both)]
            for row, slot_row, count in pieces:
                if count:
                    landing = pl.ds(slot_row * SUBLANES, count * SUBLANES)
                    copies.append(
                        send(
                            grads.at[mine, part, span(row, count)],
                            grp_recv.at[chunk, part, step - 1, landing],
                            (blk, peer),
                        )
                    )
        yield
        for copy in copies:
            copy.wait_recv()
        copies = []
        if grp_each:
            row = base + grp * grp_each
            summed(part, chunk, row, 0, grp_each)
            ref = result.at[mine, part, span(row, grp_each)]
            for step in range(1, m):
                copies.append(send(ref, ref, (blk, lax.rem(grp + step, m))))
        if grp_both:
            summed(part, chunk, base + m * grp_each, grp_each, grp_both)
        yield
        for partner, first, each in reversed(history):
            for copy in copies:
                copy.wait_recv()
            copies = []
            if each:
                ref = result.at[mine, part, span(first, each)]
                copies = [send(ref, ref, partner)]
            yield
        for copy in copies:
            copy.wait_recv()
        ref = result.at[mine, part, where]
        copy = send(ref, ref, core)
        yield
        copy.wait_recv()

    relation_part(1 - mine)
    units = [
        reduce_unit(part, chunk, start, tiles)
        for chunk, (start, tiles) in enumerate(chunks_of(width))
        for part in range(2)
    ]
    for unit in units:
        next(unit)
    relation_part(mine)
    new_source, new_sums = source_step()
    source_out[0] = new_source
    source_state_out[...] = new_sums
    for unit in units:
        next(unit)
    new_target, new_target_sums = target_step()
    target_out[0] = new_target
    target_state_out[...] = new_target_sums
    while units:
        units = [unit for unit in units if next(unit, done) is not done]
    for side in range(2):
        for part in range(2):
            lanes = slice((2 * side + part) * quarter, (2 * side + part + 1) * quarter)
            fresh, sums = adagrad(
                relation_ref[:, lanes], relation_state_ref[:, lanes], result[side, part]
            )
            relation_out[:, lanes] = fresh
            relation_state_out[:, lanes] = sums
    for copy in started:
        if id(copy) not in sent:
            copy.wait_send()


def store(*refs):
    copies = [
        pltpu.make_async_copy(refs[number], refs[6 + number], refs[12].at[number])
        for number in range(6)
    ]
    for copy in copies:
        copy.start()
    for copy in copies:
        copy.wait()


def on_device(n, m, *arrays):
    arrays = list(arrays)
    rounds, slots = arrays[6].shape[0], arrays[6].shape[3]
    kinds, width = arrays[4].shape
    rows = arrays[0].shape[1]
    arrays[0] = jnp.swapaxes(arrays[0], 1, 2)
    arrays[2] = jnp.swapaxes(arrays[2], 1, 2)
    arrays[4] = arrays[4].T
    arrays[5] = arrays[5].reshape(1, kinds)
    arrays[9] = jnp.transpose(arrays[9], (1, 2, 0))
    quarter = kinds // 4
    chunks = chunks_of(width)
    plans = [plan(n, m, tiles) for _, tiles in chunks]
    copies = copy_count(n, m, width, rounds)
    largest = SUBLANES * max(sum(steps[0]) for steps, _ in plans)
    spread = SUBLANES * max(sum(last) for _, last in plans)
    slab = (max(rounds - 1, 1), width + SUBLANES, rows)
    vmem = pl.BlockSpec(memory_space=pltpu.VMEM)
    hbm = pl.BlockSpec(memory_space=pltpu.HBM)
    staged = [pltpu.VMEM(a.shape, a.dtype) for a in arrays]
    staged[9] = pltpu.SMEM(arrays[9].shape, arrays[9].dtype)
    shapes = [jax.ShapeDtypeStruct(a.shape, F32) for a in arrays[:6]]
    arrays = [pltpu.with_memory_space_constraint(a, pltpu.HBM) for a in arrays]
    outs = pl.pallas_call(
        functools.partial(kernel, n, m),
        out_shape=shapes,
        in_specs=[hbm] * 11,
        out_specs=[vmem] * 6,
        scratch_shapes=staged
        + [
            pltpu.VMEM((rounds, kinds, slots), BF16),
            pltpu.VMEM((2, 2, width, quarter), F32),
            pltpu.VMEM((2, 2, width, quarter), F32),
            pltpu.VMEM(slab, F32),
            pltpu.VMEM(slab, F32),
            pltpu.VMEM((2, width, quarter), F32),
            pltpu.VMEM((len(chunks), 2, len(plans[0][0]), largest, quarter), F32),
            pltpu.VMEM((len(chunks), 2, m - 1, spread, quarter), F32),
            pltpu.SemaphoreType.DMA((copies,)),
            pltpu.SemaphoreType.DMA((copies,)),
            pltpu.SemaphoreType.DMA((11,)),
        ],
        compiler_params=pltpu.CompilerParams(
            collective_id=0, has_side_effects=True, vmem_limit_bytes=40 * 2**20
        ),
        name="train",
    )(*arrays)
    outs = pl.pallas_call(
        store,
        out_shape=shapes,
        in_specs=[vmem] * 6,
        out_specs=[hbm] * 6,
        scratch_shapes=[pltpu.SemaphoreType.DMA((6,))],
        name="store",
    )(*outs)
    return (
        jnp.swapaxes(outs[0], 1, 2),
        outs[1],
        jnp.swapaxes(outs[2], 1, 2),
        outs[3],
        outs[4].T,
        outs[5].reshape(kinds),
    )


def solution(mesh):
    n, m = mesh.shape["blk"], mesh.shape["grp"]
    in_specs = (
        P("blk", "grp", None),
        P("blk", "grp"),
        P("blk", "grp", None),
        P("blk", "grp"),
        P(),
        P(),
        P(None, "blk", "grp", None),
        P(None, "blk", "grp", None),
        P(None, "blk", "grp", None),
        P(None, "blk", "grp"),
        P(None, "blk", "grp", None, None),
    )
    out_specs = (
        P("blk", "grp", None),
        P("blk", "grp"),
        P("blk", "grp", None),
        P("blk", "grp"),
        P(),
        P(),
    )
    return jax.shard_map(
        functools.partial(on_device, n, m),
        mesh=mesh,
        in_specs=in_specs,
        out_specs=out_specs,
        check_vma=False,
    )
```

```python
import functools

import jax
import jax.numpy as jnp
from jax import lax
from jax.experimental import pallas as pl
from jax.experimental.pallas import tpu as pltpu
from jax.sharding import PartitionSpec as P

RATE = 0.1
SUBLANES = 8
MESH = pl.DeviceIdType.MESH
BF16 = jnp.bfloat16
F32 = jnp.float32


def halves_of(x):
    high = x.astype(BF16)
    return high, (x - high.astype(F32)).astype(BF16)


def mm(a, b):
    return jnp.dot(a, b, preferred_element_type=F32)


def mm_nt(a, b):
    return lax.dot_general(a, b, (((1,), (1,)), ((), ())), preferred_element_type=F32)


def adagrad(weights, sums, grads):
    fresh = sums + jnp.sum(grads * grads, axis=0, keepdims=True) * (1.0 / grads.shape[0])
    return weights - RATE * grads * lax.rsqrt(fresh), fresh


def chunks_of(width):
    tiles = width // SUBLANES
    large = 1 << (tiles.bit_length() - 1)
    return [(0, large), (large, tiles - large)] if large < tiles else [(0, tiles)]


def plan(n, m, tiles):
    steps = []
    for _ in range(1, n.bit_length() - 1):
        each, both = tiles // 2, tiles % 2
        steps.append((each, both))
        tiles = each + both
    return steps, (tiles // m, tiles % m)


def copy_count(n, m, width, rounds):
    count = rounds - 1
    for _, tiles in chunks_of(width):
        steps, (each, both) = plan(n, m, tiles)
        unit = 2 + len(steps) + sum(1 for step in steps if step[0])
        unit += (m - 1) * (2 * (each > 0) + (both > 0))
        count += 2 * unit
    return count


def kernel(n, m, *refs):
    hbm, refs = refs[:11], refs[11:]
    outs, refs = refs[:6], refs[6:]
    staged, refs = refs[:11], refs[11:]
    inner(n, m, hbm, *staged, *outs, *refs)


def inner(
    n,
    m,
    hbm,
    source_ref,
    source_state_ref,
    target_ref,
    target_state_ref,
    relation_ref,
    relation_state_ref,
    source_ids_ref,
    target_ids_ref,
    relation_ids_ref,
    counts_ref,
    samples_ref,
    source_out,
    source_state_out,
    target_out,
    target_state_out,
    relation_out,
    relation_state_out,
    hot_ref,
    grads,
    result,
    slab_send,
    slab_recv,
    first_recv,
    step_recv,
    grp_recv,
    send_sem,
    recv_sem,
    load_sem,
):
    staged = (
        source_ref,
        source_state_ref,
        target_ref,
        target_state_ref,
        relation_ref,
        relation_state_ref,
        source_ids_ref,
        target_ids_ref,
        relation_ids_ref,
        counts_ref,
        samples_ref,
    )
    loads = [
        pltpu.make_async_copy(src, dst, load_sem.at[number])
        for number, (src, dst) in enumerate(zip(hbm, staged))
    ]
    for number in (4, 8, 0, 6, 2, 7, 10, 9, 1, 3, 5):
        loads[number].start()
    blk, grp = lax.axis_index("blk"), lax.axis_index("grp")
    bits = n.bit_length() - 1
    rounds = source_ids_ref.shape[0]
    slots = source_ids_ref.shape[3]
    samples = samples_ref.shape[4]
    width, rows = source_ref.shape[1:]
    kinds = relation_ref.shape[1]
    quarter = kinds // 4
    after, before = lax.rem(blk + 1, n), lax.rem(blk + n - 1, n)

    def bit_of(bit):
        return lax.rem(blk // (1 << bit), 2)

    def flipped(bit):
        return blk + (1 << bit) - 2 * (1 << bit) * bit_of(bit)

    barrier = pltpu.get_barrier_semaphore()
    greeted = [(after, grp), (before, grp)]
    greeted += [(flipped(bit), grp) for bit in range(bits)]
    greeted += [(blk, lax.rem(grp + step, m)) for step in range(1, m)]
    for where in greeted:
        pl.semaphore_signal(barrier, inc=1, device_id=where, device_id_type=MESH)

    started, sent = [], []

    def send(src, dst, where):
        copy = pltpu.make_async_remote_copy(
            src_ref=src,
            dst_ref=dst,
            send_sem=send_sem.at[len(started)],
            recv_sem=recv_sem.at[len(started)],
            device_id=where,
            device_id_type=MESH,
        )
        copy.start()
        started.append(copy)
        return copy

    loads[4].wait()
    table_high, table_low = halves_of(relation_ref[...])

    def relation_side(index):
        picked = relation_ids_ref[index, 0]
        hot = (lax.broadcasted_iota(jnp.int32, (kinds, slots), 0) == picked).astype(BF16)
        hot_ref[index] = hot
        return mm(table_high, hot) + mm(table_low, hot)

    def edge_side(index):
        row_iota = lax.broadcasted_iota(jnp.int32, (rows, slots), 0)
        source_hot = (row_iota == source_ids_ref[index, 0]).astype(BF16)
        target_hot = row_iota == target_ids_ref[index, 0]
        sample_iota = lax.broadcasted_iota(jnp.int32, (rows, samples), 0)
        named = (sample_iota == samples_ref[index, 0, 0]).astype(F32)
        share = jnp.sum(named, axis=1, keepdims=True) * (1.0 / samples)
        alive = (
            lax.broadcasted_iota(jnp.int32, (1, slots), 1) < counts_ref[0, 0, index]
        ).astype(F32)
        return source_hot, target_hot, share, alive

    loads[8].wait()
    scale = relation_side(0)
    for number in (0, 6, 2, 7, 10, 9, 1, 3, 5):
        loads[number].wait()
    source, source_sums = source_ref[0], source_state_ref[...]
    target, target_sums = target_ref[0], target_state_ref[...]
    edges = edge_side(0)
    pl.semaphore_wait(barrier, len(greeted))

    for index in range(rounds):
        source_hot, target_hot, share, alive = edges
        source_high, source_low = halves_of(source)
        left = mm(
            jnp.concatenate([source_high, source_low], axis=1),
            jnp.concatenate([source_hot, source_hot], axis=0),
        )
        query = left * scale
        query_high, query_low = halves_of(query)
        flat_high, flat_low = halves_of(target.T)
        both = mm(jnp.concatenate([flat_high, flat_low], axis=0), query_high)
        logits = both[:rows] + (both[rows:] + mm(flat_high, query_low))
        positive = jnp.sum(jnp.where(target_hot, logits, 0.0), axis=0, keepdims=True)
        pull = -alive * jax.nn.sigmoid(-positive)
        push = share * alive * jax.nn.sigmoid(logits)
        weight = jnp.where(target_hot, pull, 0.0) + push
        weight_high, weight_low = halves_of(weight)
        target_high, target_low = halves_of(target)
        grad_query = mm(
            jnp.concatenate([target_high, target_low, target_high], axis=1),
            jnp.concatenate([weight_high, weight_high, weight_low], axis=0),
        )

        def source_step():
            high, low = halves_of(grad_query * scale)
            fresh = mm_nt(high, source_hot) + mm_nt(low, source_hot)
            return adagrad(source, source_sums, fresh)

        def target_step():
            pair = mm_nt(query_high, jnp.concatenate([weight_high, weight_low], axis=0))
            fresh = pair[:, :rows] + (pair[:, rows:] + mm_nt(query_low, weight_high))
            return adagrad(target, target_sums, fresh)

        relation_high, relation_low = halves_of(grad_query * left)

        def relation_part(core):
            hot = hot_ref[index, pl.ds(pl.multiple_of(core * 2 * quarter, quarter), 2 * quarter)]
            fresh = mm_nt(relation_high, hot) + mm_nt(relation_low, hot)
            for part in range(2):
                piece = fresh[:, part * quarter : (part + 1) * quarter]
                if index == 0:
                    grads[core, part] = piece
                else:
                    grads[core, part] += piece

        if index + 1 < rounds:
            new_source, new_sums = source_step()
            slab_send[index, :width] = new_source
            slab_send[index, width:] = jnp.broadcast_to(new_sums, (SUBLANES, rows))
            copy = send(slab_send.at[index], slab_recv.at[index], (after, grp))
            new_target, new_target_sums = target_step()
            relation_part(0)
            relation_part(1)
            scale = relation_side(index + 1)
            edges = edge_side(index + 1)
            target, target_sums = new_target, new_target_sums
            copy.wait_recv()
            source = slab_recv[index, :width]
            source_sums = slab_recv[index, width : width + 1]

    mine = bit_of(0)
    core = (flipped(0), grp)
    orders = [list(range(1, bits)), list(range(bits - 1, 0, -1))]

    def span(base, tiles):
        return pl.ds(pl.multiple_of(base * SUBLANES, SUBLANES), tiles * SUBLANES)

    def summed(part, chunk, base, first, tiles):
        own = grads[mine, part, span(base, tiles)]
        total = None
        for member in range(m):
            slot = lax.max(lax.rem(grp - member + m, m) - 1, 0)
            came = grp_recv[
                chunk, part, slot, first * SUBLANES : (first + tiles) * SUBLANES
            ]
            term = jnp.where(grp == member, own, came)
            total = term if total is None else total + term
        result[mine, part, span(base, tiles)] = total

    def reduce_unit(part, chunk, start, tiles):
        steps, (grp_each, grp_both) = plan(n, m, tiles)
        where = span(start, tiles)
        copy = send(
            grads.at[1 - mine, part, where], first_recv.at[part, where], core
        )
        yield
        copy.wait_recv()
        grads[mine, part, where] += first_recv[part, where]
        base, history = start, []
        for number, (each, both) in enumerate(steps):
            bit = orders[part][number]
            high = bit_of(bit)
            partner = (flipped(bit), grp)
            size = each + both
            copy = send(
                grads.at[mine, part, span(base + (1 - high) * each, size)],
                step_recv.at[chunk, part, number, pl.ds(0, size * SUBLANES)],
                partner,
            )
            history.append((partner, base + high * size, each))
            base = base + high * each
            yield
            copy.wait_recv()
            if both:
                copy.wait_send()
                sent.append(id(copy))
            came = step_recv[chunk, part, number, : size * SUBLANES]
            grads[mine, part, span(base, size)] += came
        copies = []
        for step in range(1, m):
            peer = lax.rem(grp + step, m)
            pieces = [(base + peer * grp_each, 0, grp_each)]
            pieces += [(base + m * grp_each, grp_each, grp_both)]
            for row, slot_row, count in pieces:
                if count:
                    landing = pl.ds(slot_row * SUBLANES, count * SUBLANES)
                    copies.append(
                        send(
                            grads.at[mine, part, span(row, count)],
                            grp_recv.at[chunk, part, step - 1, landing],
                            (blk, peer),
                        )
                    )
        yield
        for copy in copies:
            copy.wait_recv()
        copies = []
        if grp_each:
            row = base + grp * grp_each
            summed(part, chunk, row, 0, grp_each)
            ref = result.at[mine, part, span(row, grp_each)]
            for step in range(1, m):
                copies.append(send(ref, ref, (blk, lax.rem(grp + step, m))))
        if grp_both:
            summed(part, chunk, base + m * grp_each, grp_each, grp_both)
        yield
        for partner, first, each in reversed(history):
            for copy in copies:
                copy.wait_recv()
            copies = []
            if each:
                ref = result.at[mine, part, span(first, each)]
                copies = [send(ref, ref, partner)]
            yield
        for copy in copies:
            copy.wait_recv()
        ref = result.at[mine, part, where]
        copy = send(ref, ref, core)
        yield
        copy.wait_recv()

    relation_part(1 - mine)
    units = [
        reduce_unit(part, chunk, start, tiles)
        for chunk, (start, tiles) in enumerate(chunks_of(width))
        for part in range(2)
    ]
    for unit in units:
        next(unit)
    relation_part(mine)
    new_source, new_sums = source_step()
    source_out[0] = new_source
    source_state_out[...] = new_sums
    for unit in units:
        next(unit)
    new_target, new_target_sums = target_step()
    target_out[0] = new_target
    target_state_out[...] = new_target_sums
    for _ in range(2 * (bits - 1) + 2):
        for unit in units:
            next(unit)

    def relation_step(side, part):
        lanes = pl.ds(pl.multiple_of((2 * side + part) * quarter, quarter), quarter)
        fresh, sums = adagrad(
            relation_ref[:, lanes], relation_state_ref[:, lanes], result[side, part]
        )
        relation_out[:, lanes] = fresh
        relation_state_out[:, lanes] = sums

    for part in range(2):
        relation_step(mine, part)
    for unit in units:
        next(unit, None)
    for part in range(2):
        relation_step(1 - mine, part)
    for copy in started:
        if id(copy) not in sent:
            copy.wait_send()


def store(*refs):
    copies = [
        pltpu.make_async_copy(refs[number], refs[6 + number], refs[12].at[number])
        for number in range(6)
    ]
    for copy in copies:
        copy.start()
    for copy in copies:
        copy.wait()


def on_device(n, m, *arrays):
    arrays = list(arrays)
    rounds, slots = arrays[6].shape[0], arrays[6].shape[3]
    kinds, width = arrays[4].shape
    rows = arrays[0].shape[1]
    arrays[0] = jnp.swapaxes(arrays[0], 1, 2)
    arrays[2] = jnp.swapaxes(arrays[2], 1, 2)
    arrays[4] = arrays[4].T
    arrays[5] = arrays[5].reshape(1, kinds)
    arrays[9] = jnp.transpose(arrays[9], (1, 2, 0))
    quarter = kinds // 4
    chunks = chunks_of(width)
    plans = [plan(n, m, tiles) for _, tiles in chunks]
    copies = copy_count(n, m, width, rounds)
    largest = SUBLANES * max(sum(steps[0]) for steps, _ in plans)
    spread = SUBLANES * max(sum(last) for _, last in plans)
    slab = (max(rounds - 1, 1), width + SUBLANES, rows)
    vmem = pl.BlockSpec(memory_space=pltpu.VMEM)
    hbm = pl.BlockSpec(memory_space=pltpu.HBM)
    staged = [pltpu.VMEM(a.shape, a.dtype) for a in arrays]
    staged[9] = pltpu.SMEM(arrays[9].shape, arrays[9].dtype)
    shapes = [jax.ShapeDtypeStruct(a.shape, F32) for a in arrays[:6]]
    arrays = [pltpu.with_memory_space_constraint(a, pltpu.HBM) for a in arrays]
    outs = pl.pallas_call(
        functools.partial(kernel, n, m),
        out_shape=[pltpu.VMEM(a.shape, F32) for a in arrays[:6]],
        in_specs=[hbm] * 11,
        out_specs=[vmem] * 6,
        scratch_shapes=staged
        + [
            pltpu.VMEM((rounds, kinds, slots), BF16),
            pltpu.VMEM((2, 2, width, quarter), F32),
            pltpu.VMEM((2, 2, width, quarter), F32),
            pltpu.VMEM(slab, F32),
            pltpu.VMEM(slab, F32),
            pltpu.VMEM((2, width, quarter), F32),
            pltpu.VMEM((len(chunks), 2, len(plans[0][0]), largest, quarter), F32),
            pltpu.VMEM((len(chunks), 2, m - 1, spread, quarter), F32),
            pltpu.SemaphoreType.DMA((copies,)),
            pltpu.SemaphoreType.DMA((copies,)),
            pltpu.SemaphoreType.DMA((11,)),
        ],
        compiler_params=pltpu.CompilerParams(
            collective_id=0, has_side_effects=True, vmem_limit_bytes=40 * 2**20
        ),
        name="train",
    )(*arrays)
    outs = [pltpu.with_memory_space_constraint(a, pltpu.VMEM) for a in outs]
    outs = pl.pallas_call(
        store,
        out_shape=shapes,
        in_specs=[vmem] * 6,
        out_specs=[hbm] * 6,
        scratch_shapes=[pltpu.SemaphoreType.DMA((6,))],
        name="store",
    )(*outs)
    return (
        jnp.swapaxes(outs[0], 1, 2),
        outs[1],
        jnp.swapaxes(outs[2], 1, 2),
        outs[3],
        outs[4].T,
        outs[5].reshape(kinds),
    )


def solution(mesh):
    n, m = mesh.shape["blk"], mesh.shape["grp"]
    in_specs = (
        P("blk", "grp", None),
        P("blk", "grp"),
        P("blk", "grp", None),
        P("blk", "grp"),
        P(),
        P(),
        P(None, "blk", "grp", None),
        P(None, "blk", "grp", None),
        P(None, "blk", "grp", None),
        P(None, "blk", "grp"),
        P(None, "blk", "grp", None, None),
    )
    out_specs = (
        P("blk", "grp", None),
        P("blk", "grp"),
        P("blk", "grp", None),
        P("blk", "grp"),
        P(),
        P(),
    )
    return jax.shard_map(
        functools.partial(on_device, n, m),
        mesh=mesh,
        in_specs=in_specs,
        out_specs=out_specs,
        check_vma=False,
    )
```

```python
import functools

import jax
import jax.numpy as jnp
from jax import lax
from jax.experimental import pallas as pl
from jax.experimental.pallas import tpu as pltpu
from jax.sharding import PartitionSpec as P

RATE = 0.1
SUBLANES = 8
MESH = pl.DeviceIdType.MESH
BF16 = jnp.bfloat16
F32 = jnp.float32


def halves_of(x):
    high = x.astype(BF16)
    return high, (x - high.astype(F32)).astype(BF16)


def mm(a, b):
    return jnp.dot(a, b, preferred_element_type=F32)


def mm_nt(a, b):
    return lax.dot_general(a, b, (((1,), (1,)), ((), ())), preferred_element_type=F32)


def adagrad(weights, sums, grads):
    fresh = sums + jnp.sum(grads * grads, axis=0, keepdims=True) * (1.0 / grads.shape[0])
    return weights - RATE * grads * lax.rsqrt(fresh), fresh


def chunks_of(width):
    tiles = width // SUBLANES
    usual = max((1 << (tiles.bit_length() - 1)) // 2, 1)
    sizes = [usual] * (tiles // usual)
    sizes[0] += tiles % usual
    return [(sum(sizes[:number]), size) for number, size in enumerate(sizes)]


def plan(n, m, tiles):
    steps = []
    for _ in range(1, n.bit_length() - 1):
        each, both = tiles // 2, tiles % 2
        steps.append((each, both))
        tiles = each + both
    return steps, (tiles // m, tiles % m)


def copy_count(n, m, width, rounds):
    count = rounds - 1
    for _, tiles in chunks_of(width):
        steps, (each, both) = plan(n, m, tiles)
        unit = 2 + len(steps) + sum(1 for step in steps if step[0])
        unit += (m - 1) * (2 * (each > 0) + (both > 0))
        count += 2 * unit
    return count


def kernel(n, m, *refs):
    hbm, refs = refs[:11], refs[11:]
    outs, refs = refs[:6], refs[6:]
    staged, refs = refs[:11], refs[11:]
    inner(n, m, hbm, *staged, *outs, *refs)


def inner(
    n,
    m,
    hbm,
    source_ref,
    source_state_ref,
    target_ref,
    target_state_ref,
    relation_ref,
    relation_state_ref,
    source_ids_ref,
    target_ids_ref,
    relation_ids_ref,
    counts_ref,
    samples_ref,
    source_out,
    source_state_out,
    target_out,
    target_state_out,
    relation_out,
    relation_state_out,
    hot_ref,
    grads,
    result,
    slab_send,
    slab_recv,
    first_recv,
    step_recv,
    grp_recv,
    send_sem,
    recv_sem,
    load_sem,
):
    staged = (
        source_ref,
        source_state_ref,
        target_ref,
        target_state_ref,
        relation_ref,
        relation_state_ref,
        source_ids_ref,
        target_ids_ref,
        relation_ids_ref,
        counts_ref,
        samples_ref,
    )
    loads = [
        pltpu.make_async_copy(src, dst, load_sem.at[number])
        for number, (src, dst) in enumerate(zip(hbm, staged))
    ]
    for number in (8, 4, 6, 7, 10, 9, 0, 2, 1, 3, 5):
        loads[number].start()
    blk, grp = lax.axis_index("blk"), lax.axis_index("grp")
    bits = n.bit_length() - 1
    rounds = source_ids_ref.shape[0]
    slots = source_ids_ref.shape[3]
    samples = samples_ref.shape[4]
    width, rows = source_ref.shape[1:]
    kinds = relation_ref.shape[1]
    quarter = kinds // 4
    after, before = lax.rem(blk + 1, n), lax.rem(blk + n - 1, n)

    def bit_of(bit):
        return lax.rem(blk // (1 << bit), 2)

    def flipped(bit):
        return blk + (1 << bit) - 2 * (1 << bit) * bit_of(bit)

    barrier = pltpu.get_barrier_semaphore()
    greeted = [(after, grp), (before, grp)]
    greeted += [(flipped(bit), grp) for bit in range(bits)]
    greeted += [(blk, lax.rem(grp + step, m)) for step in range(1, m)]
    for where in greeted:
        pl.semaphore_signal(barrier, inc=1, device_id=where, device_id_type=MESH)

    started, sent = [], []

    def send(src, dst, where):
        copy = pltpu.make_async_remote_copy(
            src_ref=src,
            dst_ref=dst,
            send_sem=send_sem.at[len(started)],
            recv_sem=recv_sem.at[len(started)],
            device_id=where,
            device_id_type=MESH,
        )
        copy.start()
        started.append(copy)
        return copy

    def kinds_of(index):
        picked = relation_ids_ref[index, 0]
        hot = (lax.broadcasted_iota(jnp.int32, (kinds, slots), 0) == picked).astype(BF16)
        hot_ref[index] = hot
        return hot

    def scale_of(hot):
        return mm(table_high, hot) + mm(table_low, hot)

    def target_side(target):
        return halves_of(target), halves_of(target.T)

    def edge_side(index):
        row_iota = lax.broadcasted_iota(jnp.int32, (rows, slots), 0)
        source_hot = (row_iota == source_ids_ref[index, 0]).astype(BF16)
        target_hot = row_iota == target_ids_ref[index, 0]
        sample_iota = lax.broadcasted_iota(jnp.int32, (rows, samples), 0)
        named = (sample_iota == samples_ref[index, 0, 0]).astype(F32)
        share = jnp.sum(named, axis=1, keepdims=True) * (1.0 / samples)
        alive = (
            lax.broadcasted_iota(jnp.int32, (1, slots), 1) < counts_ref[0, 0, index]
        ).astype(F32)
        return source_hot, target_hot, share, alive

    loads[8].wait()
    hot = kinds_of(0)
    for number in (6, 7, 10, 9):
        loads[number].wait()
    edges = edge_side(0)
    loads[4].wait()
    table_high, table_low = halves_of(relation_ref[...])
    scale = scale_of(hot)
    for number in (0, 2, 1, 3, 5):
        loads[number].wait()
    source, source_sums = source_ref[0], source_state_ref[...]
    target, target_sums = target_ref[0], target_state_ref[...]
    sides = target_side(target)
    pl.semaphore_wait(barrier, len(greeted))

    for index in range(rounds):
        source_hot, target_hot, share, alive = edges
        source_high, source_low = halves_of(source)
        left = mm(
            jnp.concatenate([source_high, source_low], axis=1),
            jnp.concatenate([source_hot, source_hot], axis=0),
        )
        query = left * scale
        query_high, query_low = halves_of(query)
        (target_high, target_low), (flat_high, flat_low) = sides
        both = mm(jnp.concatenate([flat_high, flat_low], axis=0), query_high)
        logits = both[:rows] + (both[rows:] + mm(flat_high, query_low))
        positive = jnp.sum(jnp.where(target_hot, logits, 0.0), axis=0, keepdims=True)
        pull = -alive * jax.nn.sigmoid(-positive)
        push = share * alive * jax.nn.sigmoid(logits)
        weight = jnp.where(target_hot, pull, 0.0) + push
        weight_high, weight_low = halves_of(weight)
        grad_query = mm(
            jnp.concatenate([target_high, target_low, target_high], axis=1),
            jnp.concatenate([weight_high, weight_high, weight_low], axis=0),
        )

        def source_step():
            high, low = halves_of(grad_query * scale)
            fresh = mm_nt(high, source_hot) + mm_nt(low, source_hot)
            return adagrad(source, source_sums, fresh)

        def target_step():
            pair = mm_nt(query_high, jnp.concatenate([weight_high, weight_low], axis=0))
            fresh = pair[:, :rows] + (pair[:, rows:] + mm_nt(query_low, weight_high))
            return adagrad(target, target_sums, fresh)

        relation_high, relation_low = halves_of(grad_query * left)

        def relation_part(core):
            hot = hot_ref[index, pl.ds(pl.multiple_of(core * 2 * quarter, quarter), 2 * quarter)]
            fresh = mm_nt(relation_high, hot) + mm_nt(relation_low, hot)
            for part in range(2):
                piece = fresh[:, part * quarter : (part + 1) * quarter]
                if index == 0:
                    grads[core, part] = piece
                else:
                    grads[core, part] += piece

        if index + 1 < rounds:
            new_source, new_sums = source_step()
            slab_send[index, :width] = new_source
            slab_send[index, width:] = jnp.broadcast_to(new_sums, (SUBLANES, rows))
            copy = send(slab_send.at[index], slab_recv.at[index], (after, grp))
            new_target, new_target_sums = target_step()
            relation_part(0)
            relation_part(1)
            scale = scale_of(kinds_of(index + 1))
            edges = edge_side(index + 1)
            target, target_sums = new_target, new_target_sums
            sides = target_side(target)
            copy.wait_recv()
            source = slab_recv[index, :width]
            source_sums = slab_recv[index, width : width + 1]

    mine = bit_of(0)
    core = (flipped(0), grp)
    orders = [list(range(1, bits)), list(range(bits - 1, 0, -1))]

    def span(base, tiles):
        return pl.ds(pl.multiple_of(base * SUBLANES, SUBLANES), tiles * SUBLANES)

    def summed(part, chunk, base, first, tiles):
        own = grads[mine, part, span(base, tiles)]
        total = None
        for member in range(m):
            slot = lax.max(lax.rem(grp - member + m, m) - 1, 0)
            came = grp_recv[
                chunk, part, slot, first * SUBLANES : (first + tiles) * SUBLANES
            ]
            term = jnp.where(grp == member, own, came)
            total = term if total is None else total + term
        result[mine, part, span(base, tiles)] = total

    def reduce_unit(part, chunk, start, tiles):
        steps, (grp_each, grp_both) = plan(n, m, tiles)
        where = span(start, tiles)
        copy = send(
            grads.at[1 - mine, part, where], first_recv.at[part, where], core
        )
        yield
        copy.wait_recv()
        grads[mine, part, where] += first_recv[part, where]
        base, history = start, []
        for number, (each, both) in enumerate(steps):
            bit = orders[part][number]
            high = bit_of(bit)
            partner = (flipped(bit), grp)
            size = each + both
            copy = send(
                grads.at[mine, part, span(base + (1 - high) * each, size)],
                step_recv.at[chunk, part, number, pl.ds(0, size * SUBLANES)],
                partner,
            )
            history.append((partner, base + high * size, each))
            base = base + high * each
            yield
            copy.wait_recv()
            if both:
                copy.wait_send()
                sent.append(id(copy))
            came = step_recv[chunk, part, number, : size * SUBLANES]
            grads[mine, part, span(base, size)] += came
        copies = []
        for step in range(1, m):
            peer = lax.rem(grp + step, m)
            pieces = [(base + peer * grp_each, 0, grp_each)]
            pieces += [(base + m * grp_each, grp_each, grp_both)]
            for row, slot_row, count in pieces:
                if count:
                    landing = pl.ds(slot_row * SUBLANES, count * SUBLANES)
                    copies.append(
                        send(
                            grads.at[mine, part, span(row, count)],
                            grp_recv.at[chunk, part, step - 1, landing],
                            (blk, peer),
                        )
                    )
        yield
        for copy in copies:
            copy.wait_recv()
        copies = []
        if grp_each:
            row = base + grp * grp_each
            summed(part, chunk, row, 0, grp_each)
            ref = result.at[mine, part, span(row, grp_each)]
            for step in range(1, m):
                copies.append(send(ref, ref, (blk, lax.rem(grp + step, m))))
        if grp_both:
            summed(part, chunk, base + m * grp_each, grp_each, grp_both)
        yield
        for partner, first, each in reversed(history):
            for copy in copies:
                copy.wait_recv()
            copies = []
            if each:
                ref = result.at[mine, part, span(first, each)]
                copies = [send(ref, ref, partner)]
            yield
        for copy in copies:
            copy.wait_recv()
        ref = result.at[mine, part, where]
        copy = send(ref, ref, core)
        yield
        copy.wait_recv()

    relation_part(1 - mine)
    units = [
        reduce_unit(part, chunk, start, tiles)
        for chunk, (start, tiles) in enumerate(chunks_of(width))
        for part in range(2)
    ]
    for unit in units:
        next(unit)
    relation_part(mine)
    for unit in units:
        next(unit)
    new_source, new_sums = source_step()
    source_out[0] = new_source
    source_state_out[...] = new_sums
    for unit in units:
        next(unit)
    new_target, new_target_sums = target_step()
    target_out[0] = new_target
    target_state_out[...] = new_target_sums
    for _ in range(2 * (bits - 1) + 1):
        for unit in units:
            next(unit)

    def relation_step(side, part):
        lanes = pl.ds(pl.multiple_of((2 * side + part) * quarter, quarter), quarter)
        fresh, sums = adagrad(
            relation_ref[:, lanes], relation_state_ref[:, lanes], result[side, part]
        )
        relation_out[:, lanes] = fresh
        relation_state_out[:, lanes] = sums

    for part in range(2):
        relation_step(mine, part)
    for unit in units:
        next(unit, None)
    for part in range(2):
        relation_step(1 - mine, part)
    for copy in started:
        if id(copy) not in sent:
            copy.wait_send()


def store(*refs):
    copies = [
        pltpu.make_async_copy(refs[number], refs[6 + number], refs[12].at[number])
        for number in range(6)
    ]
    for copy in copies:
        copy.start()
    for copy in copies:
        copy.wait()


def on_device(n, m, *arrays):
    arrays = list(arrays)
    rounds, slots = arrays[6].shape[0], arrays[6].shape[3]
    kinds, width = arrays[4].shape
    rows = arrays[0].shape[1]
    arrays[0] = jnp.swapaxes(arrays[0], 1, 2)
    arrays[2] = jnp.swapaxes(arrays[2], 1, 2)
    arrays[4] = arrays[4].T
    arrays[5] = arrays[5].reshape(1, kinds)
    arrays[9] = jnp.transpose(arrays[9], (1, 2, 0))
    quarter = kinds // 4
    chunks = chunks_of(width)
    plans = [plan(n, m, tiles) for _, tiles in chunks]
    copies = copy_count(n, m, width, rounds)
    largest = SUBLANES * max(sum(steps[0]) for steps, _ in plans)
    spread = SUBLANES * max(sum(last) for _, last in plans)
    slab = (max(rounds - 1, 1), width + SUBLANES, rows)
    vmem = pl.BlockSpec(memory_space=pltpu.VMEM)
    hbm = pl.BlockSpec(memory_space=pltpu.HBM)
    staged = [pltpu.VMEM(a.shape, a.dtype) for a in arrays]
    staged[9] = pltpu.SMEM(arrays[9].shape, arrays[9].dtype)
    shapes = [jax.ShapeDtypeStruct(a.shape, F32) for a in arrays[:6]]
    arrays = [pltpu.with_memory_space_constraint(a, pltpu.HBM) for a in arrays]
    outs = pl.pallas_call(
        functools.partial(kernel, n, m),
        out_shape=[pltpu.VMEM(a.shape, F32) for a in arrays[:6]],
        in_specs=[hbm] * 11,
        out_specs=[vmem] * 6,
        scratch_shapes=staged
        + [
            pltpu.VMEM((rounds, kinds, slots), BF16),
            pltpu.VMEM((2, 2, width, quarter), F32),
            pltpu.VMEM((2, 2, width, quarter), F32),
            pltpu.VMEM(slab, F32),
            pltpu.VMEM(slab, F32),
            pltpu.VMEM((2, width, quarter), F32),
            pltpu.VMEM((len(chunks), 2, len(plans[0][0]), largest, quarter), F32),
            pltpu.VMEM((len(chunks), 2, m - 1, spread, quarter), F32),
            pltpu.SemaphoreType.DMA((copies,)),
            pltpu.SemaphoreType.DMA((copies,)),
            pltpu.SemaphoreType.DMA((11,)),
        ],
        compiler_params=pltpu.CompilerParams(
            collective_id=0, has_side_effects=True, vmem_limit_bytes=40 * 2**20
        ),
        name="train",
    )(*arrays)
    outs = [pltpu.with_memory_space_constraint(a, pltpu.VMEM) for a in outs]
    outs = pl.pallas_call(
        store,
        out_shape=shapes,
        in_specs=[vmem] * 6,
        out_specs=[hbm] * 6,
        scratch_shapes=[pltpu.SemaphoreType.DMA((6,))],
        name="store",
    )(*outs)
    return (
        jnp.swapaxes(outs[0], 1, 2),
        outs[1],
        jnp.swapaxes(outs[2], 1, 2),
        outs[3],
        outs[4].T,
        outs[5].reshape(kinds),
    )


def solution(mesh):
    n, m = mesh.shape["blk"], mesh.shape["grp"]
    in_specs = (
        P("blk", "grp", None),
        P("blk", "grp"),
        P("blk", "grp", None),
        P("blk", "grp"),
        P(),
        P(),
        P(None, "blk", "grp", None),
        P(None, "blk", "grp", None),
        P(None, "blk", "grp", None),
        P(None, "blk", "grp"),
        P(None, "blk", "grp", None, None),
    )
    out_specs = (
        P("blk", "grp", None),
        P("blk", "grp"),
        P("blk", "grp", None),
        P("blk", "grp"),
        P(),
        P(),
    )
    return jax.shard_map(
        functools.partial(on_device, n, m),
        mesh=mesh,
        in_specs=in_specs,
        out_specs=out_specs,
        check_vma=False,
    )
```

```python
import functools

import jax
import jax.numpy as jnp
from jax import lax
from jax.experimental import pallas as pl
from jax.experimental.pallas import tpu as pltpu
from jax.sharding import PartitionSpec as P

RATE = 0.1
SUBLANES = 8
MESH = pl.DeviceIdType.MESH
BF16 = jnp.bfloat16
F32 = jnp.float32


def halves_of(x):
    high = x.astype(BF16)
    return high, (x - high.astype(F32)).astype(BF16)


def mm(a, b):
    return jnp.dot(a, b, preferred_element_type=F32)


def mm_nt(a, b):
    return lax.dot_general(a, b, (((1,), (1,)), ((), ())), preferred_element_type=F32)


def adagrad(weights, sums, grads):
    fresh = sums + jnp.sum(grads * grads, axis=0, keepdims=True) * (1.0 / grads.shape[0])
    return weights - RATE * grads * lax.rsqrt(fresh), fresh


def chunks_of(width):
    tiles = width // SUBLANES
    usual = max((1 << (tiles.bit_length() - 1)) // 2, 1)
    sizes = [usual] * (tiles // usual)
    sizes[0] += tiles % usual
    return [(sum(sizes[:number]), size) for number, size in enumerate(sizes)]


def plan(n, m, tiles):
    steps = []
    for _ in range(1, n.bit_length() - 1):
        each, both = tiles // 2, tiles % 2
        steps.append((each, both))
        tiles = each + both
    return steps, (tiles // m, tiles % m)


def copy_count(n, m, width, rounds):
    count = rounds - 1
    for _, tiles in chunks_of(width):
        steps, (each, both) = plan(n, m, tiles)
        unit = 2 + len(steps) + sum(1 for step in steps if step[0])
        unit += (m - 1) * (2 * (each > 0) + (both > 0))
        count += 2 * unit
    return count


def kernel(n, m, *refs):
    hbm, refs = refs[:11], refs[11:]
    outs, refs = refs[:6], refs[6:]
    staged, refs = refs[:11], refs[11:]
    inner(n, m, hbm, *staged, *outs, *refs)


def inner(
    n,
    m,
    hbm,
    source_ref,
    source_state_ref,
    target_ref,
    target_state_ref,
    relation_ref,
    relation_state_ref,
    source_ids_ref,
    target_ids_ref,
    relation_ids_ref,
    counts_ref,
    samples_ref,
    source_out,
    source_state_out,
    target_out,
    target_state_out,
    relation_out,
    relation_state_out,
    hot_ref,
    grads,
    result,
    slab_send,
    slab_recv,
    first_recv,
    step_recv,
    grp_recv,
    send_sem,
    recv_sem,
    load_sem,
):
    staged = (
        source_ref,
        source_state_ref,
        target_ref,
        target_state_ref,
        relation_ref,
        relation_state_ref,
        source_ids_ref,
        target_ids_ref,
        relation_ids_ref,
        counts_ref,
        samples_ref,
    )
    loads = [
        pltpu.make_async_copy(src, dst, load_sem.at[number])
        for number, (src, dst) in enumerate(zip(hbm, staged))
    ]
    for number in (8, 4, 6, 7, 10, 9, 0, 2, 1, 3, 5):
        loads[number].start()
    blk, grp = lax.axis_index("blk"), lax.axis_index("grp")
    bits = n.bit_length() - 1
    rounds = source_ids_ref.shape[0]
    slots = source_ids_ref.shape[3]
    samples = samples_ref.shape[4]
    width, rows = source_ref.shape[1:]
    kinds = relation_ref.shape[1]
    quarter = kinds // 4
    after, before = lax.rem(blk + 1, n), lax.rem(blk + n - 1, n)

    def bit_of(bit):
        return lax.rem(blk // (1 << bit), 2)

    def flipped(bit):
        return blk + (1 << bit) - 2 * (1 << bit) * bit_of(bit)

    barrier = pltpu.get_barrier_semaphore()
    greeted = [(after, grp), (before, grp)]
    greeted += [(flipped(bit), grp) for bit in range(bits)]
    greeted += [(blk, lax.rem(grp + step, m)) for step in range(1, m)]
    for where in greeted:
        pl.semaphore_signal(barrier, inc=1, device_id=where, device_id_type=MESH)

    started, sent = [], []

    def send(src, dst, where):
        copy = pltpu.make_async_remote_copy(
            src_ref=src,
            dst_ref=dst,
            send_sem=send_sem.at[len(started)],
            recv_sem=recv_sem.at[len(started)],
            device_id=where,
            device_id_type=MESH,
        )
        copy.start()
        started.append(copy)
        return copy

    def kinds_of(index):
        picked = relation_ids_ref[index, 0]
        hot = (lax.broadcasted_iota(jnp.int32, (kinds, slots), 0) == picked).astype(BF16)
        hot_ref[index] = hot
        return hot

    def scale_of(hot):
        pair = mm(table_pair, hot)
        return pair[:width] + pair[width:]

    def target_side(target):
        return halves_of(target), halves_of(target.T)

    def edge_side(index):
        row_iota = lax.broadcasted_iota(jnp.int32, (rows, slots), 0)
        source_hot = (row_iota == source_ids_ref[index, 0]).astype(BF16)
        target_hot = row_iota == target_ids_ref[index, 0]
        sample_iota = lax.broadcasted_iota(jnp.int32, (rows, samples), 0)
        named = (sample_iota == samples_ref[index, 0, 0]).astype(F32)
        share = jnp.sum(named, axis=1, keepdims=True) * (1.0 / samples)
        alive = (
            lax.broadcasted_iota(jnp.int32, (1, slots), 1) < counts_ref[0, 0, index]
        ).astype(F32)
        return source_hot, target_hot, share, alive

    loads[8].wait()
    hot = kinds_of(0)
    for number in (6, 7, 10, 9):
        loads[number].wait()
    edges = edge_side(0)
    loads[4].wait()
    table_pair = jnp.concatenate(halves_of(relation_ref[...]), axis=0)
    scale = scale_of(hot)
    for number in (0, 2, 1, 3, 5):
        loads[number].wait()
    source, source_sums = source_ref[0], source_state_ref[...]
    target, target_sums = target_ref[0], target_state_ref[...]
    sides = target_side(target)
    pl.semaphore_wait(barrier, len(greeted))

    for index in range(rounds):
        source_hot, target_hot, share, alive = edges
        source_high, source_low = halves_of(source)
        left = mm(
            jnp.concatenate([source_high, source_low], axis=1),
            jnp.concatenate([source_hot, source_hot], axis=0),
        )
        query = left * scale
        query_high, query_low = halves_of(query)
        (target_high, target_low), (flat_high, flat_low) = sides
        both = mm(jnp.concatenate([flat_high, flat_low], axis=0), query_high)
        logits = both[:rows] + (both[rows:] + mm(flat_high, query_low))
        positive = jnp.sum(jnp.where(target_hot, logits, 0.0), axis=0, keepdims=True)
        pull = -alive * jax.nn.sigmoid(-positive)
        push = share * alive * jax.nn.sigmoid(logits)
        weight = jnp.where(target_hot, pull, 0.0) + push
        weight_high, weight_low = halves_of(weight)
        grad_query = mm(
            jnp.concatenate([target_high, target_low, target_high], axis=1),
            jnp.concatenate([weight_high, weight_high, weight_low], axis=0),
        )

        def source_step():
            pair = jnp.concatenate(halves_of(grad_query * scale), axis=0)
            pair = mm_nt(pair, source_hot)
            fresh = pair[:width] + pair[width:]
            return adagrad(source, source_sums, fresh)

        def target_step():
            pair = mm_nt(query_high, jnp.concatenate([weight_high, weight_low], axis=0))
            fresh = pair[:, :rows] + (pair[:, rows:] + mm_nt(query_low, weight_high))
            return adagrad(target, target_sums, fresh)

        relation_pair = jnp.concatenate(halves_of(grad_query * left), axis=0)

        def relation_part(core):
            hot = hot_ref[index, pl.ds(pl.multiple_of(core * 2 * quarter, quarter), 2 * quarter)]
            pair = mm_nt(relation_pair, hot)
            fresh = pair[:width] + pair[width:]
            for part in range(2):
                piece = fresh[:, part * quarter : (part + 1) * quarter]
                if index == 0:
                    grads[core, part] = piece
                else:
                    grads[core, part] += piece

        if index + 1 < rounds:
            new_source, new_sums = source_step()
            slab_send[index, :width] = new_source
            slab_send[index, width:] = jnp.broadcast_to(new_sums, (SUBLANES, rows))
            copy = send(slab_send.at[index], slab_recv.at[index], (after, grp))
            new_target, new_target_sums = target_step()
            relation_part(0)
            relation_part(1)
            scale = scale_of(kinds_of(index + 1))
            edges = edge_side(index + 1)
            target, target_sums = new_target, new_target_sums
            sides = target_side(target)
            copy.wait_recv()
            source = slab_recv[index, :width]
            source_sums = slab_recv[index, width : width + 1]

    mine = bit_of(0)
    core = (flipped(0), grp)
    orders = [list(range(1, bits)), list(range(bits - 1, 0, -1))]

    def span(base, tiles):
        return pl.ds(pl.multiple_of(base * SUBLANES, SUBLANES), tiles * SUBLANES)

    def summed(part, chunk, base, first, tiles):
        own = grads[mine, part, span(base, tiles)]
        total = None
        for member in range(m):
            slot = lax.max(lax.rem(grp - member + m, m) - 1, 0)
            came = grp_recv[
                chunk, part, slot, first * SUBLANES : (first + tiles) * SUBLANES
            ]
            term = jnp.where(grp == member, own, came)
            total = term if total is None else total + term
        result[mine, part, span(base, tiles)] = total

    def reduce_unit(part, chunk, start, tiles):
        steps, (grp_each, grp_both) = plan(n, m, tiles)
        where = span(start, tiles)
        copy = send(
            grads.at[1 - mine, part, where], first_recv.at[part, where], core
        )
        yield
        copy.wait_recv()
        grads[mine, part, where] += first_recv[part, where]
        base, history = start, []
        for number, (each, both) in enumerate(steps):
            bit = orders[part][number]
            high = bit_of(bit)
            partner = (flipped(bit), grp)
            size = each + both
            copy = send(
                grads.at[mine, part, span(base + (1 - high) * each, size)],
                step_recv.at[chunk, part, number, pl.ds(0, size * SUBLANES)],
                partner,
            )
            history.append((partner, base + high * size, each))
            base = base + high * each
            yield
            copy.wait_recv()
            if both:
                copy.wait_send()
                sent.append(id(copy))
            came = step_recv[chunk, part, number, : size * SUBLANES]
            grads[mine, part, span(base, size)] += came
        copies = []
        for step in range(1, m):
            peer = lax.rem(grp + step, m)
            pieces = [(base + peer * grp_each, 0, grp_each)]
            pieces += [(base + m * grp_each, grp_each, grp_both)]
            for row, slot_row, count in pieces:
                if count:
                    landing = pl.ds(slot_row * SUBLANES, count * SUBLANES)
                    copies.append(
                        send(
                            grads.at[mine, part, span(row, count)],
                            grp_recv.at[chunk, part, step - 1, landing],
                            (blk, peer),
                        )
                    )
        yield
        for copy in copies:
            copy.wait_recv()
        copies = []
        if grp_each:
            row = base + grp * grp_each
            summed(part, chunk, row, 0, grp_each)
            ref = result.at[mine, part, span(row, grp_each)]
            for step in range(1, m):
                copies.append(send(ref, ref, (blk, lax.rem(grp + step, m))))
        if grp_both:
            summed(part, chunk, base + m * grp_each, grp_each, grp_both)
        yield
        for partner, first, each in reversed(history):
            for copy in copies:
                copy.wait_recv()
            copies = []
            if each:
                ref = result.at[mine, part, span(first, each)]
                copies = [send(ref, ref, partner)]
            yield
        for copy in copies:
            copy.wait_recv()
        ref = result.at[mine, part, where]
        copy = send(ref, ref, core)
        yield
        copy.wait_recv()

    relation_part(1 - mine)
    units = [
        reduce_unit(part, chunk, start, tiles)
        for chunk, (start, tiles) in enumerate(chunks_of(width))
        for part in range(2)
    ]
    for unit in units:
        next(unit)
    relation_part(mine)
    for unit in units:
        next(unit)
    new_source, new_sums = source_step()
    source_out[0] = new_source
    source_state_out[...] = new_sums
    for unit in units:
        next(unit)
    new_target, new_target_sums = target_step()
    target_out[0] = new_target
    target_state_out[...] = new_target_sums
    for _ in range(2 * (bits - 1) + 1):
        for unit in units:
            next(unit)

    def relation_step(side, part):
        lanes = pl.ds(pl.multiple_of((2 * side + part) * quarter, quarter), quarter)
        fresh, sums = adagrad(
            relation_ref[:, lanes], relation_state_ref[:, lanes], result[side, part]
        )
        relation_out[:, lanes] = fresh
        relation_state_out[:, lanes] = sums

    for part in range(2):
        relation_step(mine, part)
    for unit in units:
        next(unit, None)
    for part in range(2):
        relation_step(1 - mine, part)
    for copy in started:
        if id(copy) not in sent:
            copy.wait_send()


def store(*refs):
    copies = [
        pltpu.make_async_copy(refs[number], refs[6 + number], refs[12].at[number])
        for number in range(6)
    ]
    for copy in copies:
        copy.start()
    for copy in copies:
        copy.wait()


def on_device(n, m, *arrays):
    arrays = list(arrays)
    rounds, slots = arrays[6].shape[0], arrays[6].shape[3]
    kinds, width = arrays[4].shape
    rows = arrays[0].shape[1]
    arrays[0] = jnp.swapaxes(arrays[0], 1, 2)
    arrays[2] = jnp.swapaxes(arrays[2], 1, 2)
    arrays[4] = arrays[4].T
    arrays[5] = arrays[5].reshape(1, kinds)
    arrays[9] = jnp.transpose(arrays[9], (1, 2, 0))
    quarter = kinds // 4
    chunks = chunks_of(width)
    plans = [plan(n, m, tiles) for _, tiles in chunks]
    copies = copy_count(n, m, width, rounds)
    largest = SUBLANES * max(sum(steps[0]) for steps, _ in plans)
    spread = SUBLANES * max(sum(last) for _, last in plans)
    slab = (max(rounds - 1, 1), width + SUBLANES, rows)
    vmem = pl.BlockSpec(memory_space=pltpu.VMEM)
    hbm = pl.BlockSpec(memory_space=pltpu.HBM)
    staged = [pltpu.VMEM(a.shape, a.dtype) for a in arrays]
    staged[9] = pltpu.SMEM(arrays[9].shape, arrays[9].dtype)
    shapes = [jax.ShapeDtypeStruct(a.shape, F32) for a in arrays[:6]]
    arrays = [pltpu.with_memory_space_constraint(a, pltpu.HBM) for a in arrays]
    outs = pl.pallas_call(
        functools.partial(kernel, n, m),
        out_shape=[pltpu.VMEM(a.shape, F32) for a in arrays[:6]],
        in_specs=[hbm] * 11,
        out_specs=[vmem] * 6,
        scratch_shapes=staged
        + [
            pltpu.VMEM((rounds, kinds, slots), BF16),
            pltpu.VMEM((2, 2, width, quarter), F32),
            pltpu.VMEM((2, 2, width, quarter), F32),
            pltpu.VMEM(slab, F32),
            pltpu.VMEM(slab, F32),
            pltpu.VMEM((2, width, quarter), F32),
            pltpu.VMEM((len(chunks), 2, len(plans[0][0]), largest, quarter), F32),
            pltpu.VMEM((len(chunks), 2, m - 1, spread, quarter), F32),
            pltpu.SemaphoreType.DMA((copies,)),
            pltpu.SemaphoreType.DMA((copies,)),
            pltpu.SemaphoreType.DMA((11,)),
        ],
        compiler_params=pltpu.CompilerParams(
            collective_id=0, has_side_effects=True, vmem_limit_bytes=40 * 2**20
        ),
        name="train",
    )(*arrays)
    outs = [pltpu.with_memory_space_constraint(a, pltpu.VMEM) for a in outs]
    outs = pl.pallas_call(
        store,
        out_shape=shapes,
        in_specs=[vmem] * 6,
        out_specs=[hbm] * 6,
        scratch_shapes=[pltpu.SemaphoreType.DMA((6,))],
        name="store",
    )(*outs)
    return (
        jnp.swapaxes(outs[0], 1, 2),
        outs[1],
        jnp.swapaxes(outs[2], 1, 2),
        outs[3],
        outs[4].T,
        outs[5].reshape(kinds),
    )


def solution(mesh):
    n, m = mesh.shape["blk"], mesh.shape["grp"]
    in_specs = (
        P("blk", "grp", None),
        P("blk", "grp"),
        P("blk", "grp", None),
        P("blk", "grp"),
        P(),
        P(),
        P(None, "blk", "grp", None),
        P(None, "blk", "grp", None),
        P(None, "blk", "grp", None),
        P(None, "blk", "grp"),
        P(None, "blk", "grp", None, None),
    )
    out_specs = (
        P("blk", "grp", None),
        P("blk", "grp"),
        P("blk", "grp", None),
        P("blk", "grp"),
        P(),
        P(),
    )
    return jax.shard_map(
        functools.partial(on_device, n, m),
        mesh=mesh,
        in_specs=in_specs,
        out_specs=out_specs,
        check_vma=False,
    )
```
